256 devices in a mesh: cent: 64 (over x, z, core), slab: 4 (over y).
Axes of the slice: x: 4, y: 4, z: 8, core: 2. Of those that a mesh axis runs over, the one named last changes fastest.
Arguments:
- vectors: bfloat16 [2048, 1024], P(('slab', 'cent')), may hold values from -12 to 12
- primary: int32 [2048], P(('slab', 'cent')), may hold values from 0 to 262143, as said below
- centroids: bfloat16 [262144, 1024], P('cent'), may hold values from -12 to 12, as said below
Outputs:
- spill_logits: bfloat16 [2048, 262144], P('slab', 'cent')
The draws below stay inside these ranges and needn't reach their ends.
Inputs may be any that keep to these rules, and one draw needn't show every extreme that they name: `centroids`: every entry of the centroid table and of the vectors lies in this range. Of the vectors that one device holds, the first has its primary centroid on the cent index half the axis away (counted round), the second on the next cent index; the others lie anywhere.
All inputs are finite; a program needn't handle non-finite values.
Results may differ from the reference program's by a relative error of at most 0.001.
Values may be sent and summed in bfloat16 or wider, within the bound.
No kernel may reach another device: no remote copies, remote signals or barrier semaphores. Data moves between devices by JAX's collectives and lax.ppermute only.
A program may use at most 64 MiB of HBM per device.

```python
import jax
import jax.numpy as jnp
from jax import lax

D = 1024
K_DEV = 4096
ROWS = 512
K = 262144
N = 2048
N_CENT = 64


def centroid_row(key, index):
    row_key = jax.random.fold_in(jax.random.fold_in(key, 50), index)
    return jax.random.truncated_normal(row_key, -6.0, 6.0, (D,), jnp.float32)


def hot_table(key):
    base_key = jax.random.fold_in(key, 77)
    picks = jax.random.permutation(jax.random.fold_in(base_key, 1), K)[:8]
    strength = jnp.array([1.0, 1.3, 1.6, 1.8], jnp.float32)
    amplitude = jnp.sqrt(4096.0 * strength / D)[:, None]
    signs = jnp.where(jax.random.bernoulli(jax.random.fold_in(base_key, 2), 0.5, (4, D)), 1.0, -1.0)
    others = jnp.where(jax.random.bernoulli(jax.random.fold_in(base_key, 3), 0.5, (4, D)), 1.0, -1.0)
    leading = amplitude * signs
    second = leading + jnp.sqrt(64.0 / D) * others
    return (picks, leading, jnp.concatenate([leading, second], axis=0))


def draw_centroids(key, part):
    shared = key
    rows = jax.vmap(lambda index: centroid_row(shared, index))(jnp.arange(K))
    picks, leading, planted = hot_table(shared)
    rows = rows.at[picks].set(planted)
    return rows.astype(jnp.bfloat16)


def draw_vectors(key, part):
    shared = key
    key = jax.random.fold_in(key, 5)
    values = jax.random.truncated_normal(key, -6.0, 6.0, (N, D), jnp.float32)
    picks, leading, planted = hot_table(shared)
    index = jnp.arange(N)
    chosen = index % 16 == 3
    aligned = leading[index // 16 % 4]
    values = jnp.where(chosen[:, None], aligned, values)
    return values.astype(jnp.bfloat16)


def draw_primary(key, part):
    key = jax.random.fold_in(key, 9)
    per_device = ROWS // N_CENT
    index = jnp.arange(N, dtype=jnp.int32)
    device = index // per_device
    position = index % per_device
    column = device % N_CENT
    offsets = jax.random.randint(key, (N,), 0, N_CENT, dtype=jnp.int32)
    offsets = jnp.where(position == 0, N_CENT // 2, jnp.where(position == 1, 1, offsets))
    owner = (column + offsets) % N_CENT
    local = jax.random.randint(jax.random.fold_in(key, 1), (N,), 0, K_DEV, dtype=jnp.int32)
    return (owner * K_DEV + local).astype(jnp.int32)


def setup_inputs(seed: int = 0) -> dict:
    key_of = jax.random.split(jax.random.key(seed), 4)
    vectors = draw_vectors(jax.random.fold_in(key_of[3], 71), 0)
    primary = draw_primary(jax.random.fold_in(key_of[3], 71), 0)
    centroids = draw_centroids(jax.random.fold_in(key_of[3], 71), 0)
    return {"vectors": vectors, "primary": primary, "centroids": centroids}


def block_scores(vectors, residual, along, energy, block):
    cross = jnp.dot(vectors, block.T, preferred_element_type=jnp.float32)
    proj = jnp.dot(residual, block.T, preferred_element_type=jnp.float32)
    wide = block.astype(jnp.float32)
    norms = jnp.sum(wide * wide, axis=1)
    gap = along[:, None] - proj
    return (2.0 * cross - norms[None, :] - 1.0 * gap * gap / energy[:, None]) / 32.0


def reference(vectors, primary, centroids):
    primary_rows = jnp.take(centroids, primary.astype(jnp.int32), axis=0).astype(jnp.float32)
    residual = (vectors.astype(jnp.float32) - primary_rows).astype(jnp.bfloat16)
    wide_vec = vectors.astype(jnp.float32)
    wide_res = residual.astype(jnp.float32)
    along = jnp.sum(wide_vec * wide_res, axis=1)
    energy = 1e-6 + jnp.sum(wide_res * wide_res, axis=1)
    blocks = centroids.reshape(N_CENT, K_DEV, D)

    def accumulate(carry, block):
        peak, total = carry
        score = block_scores(vectors, residual, along, energy, block)
        newpeak = jnp.maximum(peak, jnp.max(score, axis=1))
        total = total * jnp.exp(peak - newpeak) + jnp.sum(jnp.exp(score - newpeak[:, None]), axis=1)
        return (newpeak, total), None

    start = (jnp.full((N,), -jnp.inf, jnp.float32), jnp.zeros((N,), jnp.float32))
    (peak, total), unused = lax.scan(accumulate, start, blocks)
    shift = peak + jnp.log(total) - jnp.log(jnp.float32(K))

    def finish(block):
        score = block_scores(vectors, residual, along, energy, block)
        return (score - shift[:, None]).astype(jnp.bfloat16)

    pieces = lax.map(finish, blocks)
    return jnp.transpose(pieces, (1, 0, 2)).reshape(N, K)
```

```python
import jax
import jax.numpy as jnp
from jax import lax
from jax.sharding import Mesh, PartitionSpec as P

CENT = ("x", "z", "core")
CHIPS = ("x", "z")
SWAP = [(0, 1), (1, 0)]


def broadcast_to_group(block, n):
    return jnp.broadcast_to(block[None], (n,) + block.shape)


def gather_rows(block, core):
    n = lax.axis_size(CHIPS)
    own = lax.all_to_all(broadcast_to_group(block, n), CHIPS, 0, 0, tiled=True)
    other = lax.ppermute(own, "core", SWAP)
    first = jnp.where(core == 0, own, other)
    second = jnp.where(core == 0, other, own)
    whole = jnp.stack([first, second], axis=1)
    return whole.reshape(2 * n * block.shape[0], block.shape[1])


def body(vectors, primary, centroids):
    k_dev, dim = centroids.shape
    mine = vectors.shape[0]
    owners = lax.axis_size(CENT)
    chips = lax.axis_size(CHIPS)
    core = lax.axis_index("core")
    offset = lax.axis_index(CENT) * k_dev

    ids = jnp.broadcast_to(primary[None, :, None], (owners, mine, 128))
    ids = lax.all_to_all(ids, CENT, 0, 0, tiled=True)[:, :, 0].reshape(chips, 2, mine)
    local = jnp.take(ids, jnp.stack([core, 1 - core]), axis=1) - offset
    local = jnp.swapaxes(local, 0, 1).reshape(-1)
    hot = (local[:, None] == lax.broadcasted_iota(jnp.int32, (1, k_dev), 1)).astype(jnp.bfloat16)
    found = jnp.dot(hot, centroids, preferred_element_type=jnp.float32).astype(jnp.bfloat16)
    found = found.reshape(2, chips, mine, dim)
    for_me = found[0] + lax.ppermute(found[1], "core", SWAP)
    rows = lax.all_to_all(for_me, CHIPS, 0, 0, tiled=True)
    primary_rows = jnp.sum(rows.astype(jnp.float32), axis=0)
    residual = (vectors.astype(jnp.float32) - primary_rows).astype(jnp.bfloat16)

    whole_vec = gather_rows(vectors, core)
    whole_res = gather_rows(residual, core)
    wide_vec = whole_vec.astype(jnp.float32)
    wide_res = whole_res.astype(jnp.float32)
    along = jnp.sum(wide_vec * wide_res, axis=1)
    energy = 1e-06 + jnp.sum(wide_res * wide_res, axis=1)
    norms = jnp.einsum("kd,kd->k", centroids, centroids, preferred_element_type=jnp.float32)
    cross = jnp.einsum("rd,kd->rk", whole_vec, centroids, preferred_element_type=jnp.float32)
    proj = jnp.einsum("rd,kd->rk", whole_res, centroids, preferred_element_type=jnp.float32)
    gap = along[:, None] - proj
    score = (2.0 * cross - norms[None, :] - gap * gap / energy[:, None]) / 32.0
    local_peak = jnp.max(score, axis=1)
    local_total = jnp.sum(jnp.exp(score - local_peak[:, None]), axis=1)
    lse = (local_peak + jnp.log(local_total)).reshape(-1, 128)
    every = lax.all_to_all(broadcast_to_group(lse, owners), CENT, 0, 0, tiled=True)
    peak = jnp.max(every, axis=0)
    total = jnp.sum(jnp.exp(every - peak[None]), axis=0)
    shift = (peak + jnp.log(total) - jnp.log(jnp.float32(k_dev * owners))).reshape(-1)
    return (score - shift[:, None]).astype(jnp.bfloat16)


def solution(mesh):
    fine = Mesh(mesh.devices.reshape(4, 8, 2, 4), CENT + ("slab",))
    return jax.shard_map(
        body,
        mesh=fine,
        in_specs=(P(("slab",) + CENT, None), P(("slab",) + CENT), P(CENT, None)),
        out_specs=P("slab", CENT),
        check_vma=False,
    )
```

```python
import functools

import jax
import jax.numpy as jnp
from jax import lax
from jax.experimental import pallas as pl
from jax.experimental.pallas import tpu as pltpu
from jax.sharding import Mesh, PartitionSpec as P

CENT = ("x", "z", "core")
CHIPS = ("x", "z")
SWAP = [(0, 1), (1, 0)]
F32 = jnp.float32
BF16 = jnp.bfloat16
I32 = jnp.int32
IN_VMEM = pl.BlockSpec(memory_space=pltpu.VMEM)
IN_SMEM = pl.BlockSpec(memory_space=pltpu.SMEM)
IN_PLACE = pl.BlockSpec(memory_space=pl.ANY)
PARAMS = pltpu.CompilerParams(vmem_limit_bytes=60 * 1024 * 1024)
LANES = 128
MINE = 8
STEP = 512
HALF = 16
SLOTS = 2 * HALF


def dot_t(a, b):
    return lax.dot_general(a, b, (((1,), (1,)), ((), ())), preferred_element_type=F32)


def collect_kernel(where, ids, ids_too, cent, keep, away, place, most, found, stage, spots, locals_, sems):
    k_dev, dim = cent.shape
    rows = place.shape[0]
    core = where[0]

    def scan(i, carry):
        count, pooled = carry
        owner = ids[i // MINE, 0, lax.rem(i, MINE)]
        local = owner - where[1]
        on_chip = (owner >= where[2]) & (owner < where[2] + 2 * k_dev)
        hit = (local >= 0) & (local < k_dev) & (pooled < SLOTS)
        spots[count] = pooled
        locals_[count] = local
        return count + jnp.where(hit, 1, 0), pooled + jnp.where(on_chip, 1, 0)

    count, _ = lax.fori_loop(0, rows, scan, (jnp.int32(0), jnp.int32(0)), unroll=16)

    def bring(s):
        group = pl.multiple_of(locals_[s] // 16 * 16, 16)
        return pltpu.make_async_copy(cent.at[pl.ds(group, 16), :], stage.at[s], sems.at[s])

    def start(s, carry):
        bring(s).start()
        return carry

    def take(s, carry):
        bring(s).wait()
        row = lax.broadcasted_iota(I32, (16, dim), 0)
        picked = jnp.where(row == lax.rem(locals_[s], 16), stage[s].astype(F32), 0.0)
        found[pl.ds(spots[s], 1), :] = jnp.sum(picked, axis=0, keepdims=True)
        return carry

    lax.fori_loop(0, count, start, 0)
    found[...] = jnp.zeros_like(found)

    owners = rows // MINE
    row = lax.broadcasted_iota(I32, (owners, MINE, LANES), 1)
    lane = lax.broadcasted_iota(I32, (owners, MINE, LANES), 2)
    each = jnp.broadcast_to(ids_too[...].astype(F32), (owners, MINE, LANES))
    column = jnp.sum(jnp.where(row == lane, each, 0.0), axis=2, keepdims=True).reshape(rows, 1)
    chip = jnp.broadcast_to(jnp.floor(column * (0.5 / k_dev)), (rows, LANES))
    rank = jnp.zeros((rows, LANES), F32)
    before = lax.broadcasted_iota(I32, (rows, LANES), 0)
    after = lax.broadcasted_iota(I32, (rows, LANES), 1)
    for r in range(0, rows, LANES):
        across = jnp.transpose(chip[r : r + LANES])[:1]
        rank = rank + jnp.where((chip == across) & (after + r < before), 1.0, 0.0)
    rank = jnp.sum(rank, axis=1, keepdims=True).astype(I32)
    half = lax.shift_right_logical(rank, 4) ^ core
    at = half * (rows // (2 * MINE) * HALF) + chip.astype(I32) * HALF + (rank & (HALF - 1))
    place[...] = jnp.broadcast_to(at, (rows, LANES))
    most[0] = jnp.max(rank)

    lax.fori_loop(0, count, take, 0)
    keep[...] = found[pl.ds(pl.multiple_of(core * HALF, HALF), HALF), :].astype(BF16)
    away[...] = found[pl.ds(pl.multiple_of((1 - core) * HALF, HALF), HALF), :].astype(BF16)


def score_kernel(
    pooled, where, own, other, hint, norms, cent,
    score, lse, pool, rows_of, both, table, made, held_a, held_b, stats, in_sems, out_sems,
):
    chips, _, dim = own.shape
    rows = 2 * chips * MINE
    k_dev = cent.shape[0]
    n = k_dev // STEP
    core = where[0]

    def bring(t):
        part = pl.ds(pl.multiple_of(t * STEP, STEP), STEP)
        return pltpu.make_async_copy(cent.at[part, :], table.at[part, :], in_sems.at[t])

    def give(t):
        part = pl.ds(pl.multiple_of(t * STEP, STEP), STEP)
        return pltpu.make_async_copy(made.at[:, part], score.at[:, part], out_sems.at[t])

    bring(0).start()
    bring(1).start()
    if pooled:
        for c in range(chips):
            pool[c * HALF : (c + 1) * HALF, :] = own[c, :HALF, :]
            pool[(chips + c) * HALF : (chips + c + 1) * HALF, :] = other[c, :HALF, :]
        lane = lax.broadcasted_iota(I32, (rows, LANES), 1)
        hot = [(hint[...] == lane + j).astype(F32).astype(BF16) for j in range(0, 2 * chips * HALF, LANES)]
        rows_of[...] = jnp.dot(jnp.concatenate(hot, axis=1), pool[...], preferred_element_type=F32)

    def prepare(g, carry):
        at = pl.ds(pl.multiple_of(g * 2 * MINE, 2 * MINE), 2 * MINE)
        low = pl.ds(pl.multiple_of(rows + g * 2 * MINE, 2 * MINE), 2 * MINE)
        a = own[g, HALF : HALF + MINE, :].astype(F32)
        b = other[g, HALF : HALF + MINE, :].astype(F32)
        vec = jnp.concatenate([jnp.where(core == 0, a, b), jnp.where(core == 0, b, a)], axis=0)
        near = rows_of[at, :] if pooled else hint[at, :].astype(F32)
        rounded = (vec - near).astype(BF16)
        res = rounded.astype(F32)
        both[at, :] = vec.astype(BF16)
        both[low, :] = rounded
        along = jnp.sum(vec * res, axis=1, keepdims=True)
        energy = 1e-06 + jnp.sum(res * res, axis=1, keepdims=True)
        stats[0, at, :] = jnp.broadcast_to(along, (2 * MINE, LANES))
        stats[1, at, :] = jnp.broadcast_to((1.0 / 32.0) / energy, (2 * MINE, LANES))
        return carry

    lax.fori_loop(0, chips, prepare, 0, unroll=4)
    stats[2] = jnp.full((rows, LANES), -jnp.inf, F32)
    stats[3] = jnp.zeros((rows, LANES), F32)
    held_b[...] = jnp.full_like(held_b, -1e30)
    held_b[rows:, :] = jnp.zeros((rows, STEP), F32)

    def product(held, t):
        part = pl.ds(pl.multiple_of(t * STEP, STEP), STEP)
        held[...] = dot_t(both[...], table[part, :])

    def settle(held, t):
        first = pl.multiple_of(t * STEP, STEP)
        for g in range(0, rows, 8):
            at, low = slice(g, g + 8), slice(rows + g, rows + g + 8)
            along, weight, peak = stats[0, at, :], stats[1, at, :], stats[2, at, :]
            parts = []
            for j in range(0, STEP, LANES):
                cols = pl.ds(first + j, LANES)
                gap = along - held[low, j : j + LANES]
                part = held[at, j : j + LANES] * (1.0 / 16.0) - norms[:, cols] - gap * gap * weight
                made[at, cols] = part
                parts.append(part)
            new = functools.reduce(jnp.maximum, parts, peak)
            sums = [jnp.exp(part - new) for part in parts]
            while len(sums) > 1:
                sums = [sums[i] + sums[i + 1] for i in range(0, len(sums), 2)]
            stats[3, at, :] = stats[3, at, :] * jnp.exp(peak - new) + sums[0]
            stats[2, at, :] = new

    def turn(i, carry):
        bring(2 * i).wait()
        bring(2 * i + 1).wait()

        @pl.when(i + 1 < n // 2)
        def _():
            bring(2 * i + 2).start()
            bring(2 * i + 3).start()

        product(held_a, 2 * i)
        settle(held_b, jnp.maximum(2 * i - 1, 0))
        product(held_b, 2 * i + 1)
        settle(held_a, 2 * i)

        @pl.when(i > 0)
        def _():
            give(2 * i - 1).start()

        give(2 * i).start()
        return carry

    lax.fori_loop(0, n // 2, turn, 0)
    settle(held_b, n - 1)
    give(n - 1).start()
    for r in range(0, rows, LANES):
        at = slice(r, r + LANES)
        peak = stats[2, at, :]
        top = jnp.max(peak, axis=1, keepdims=True)
        total = jnp.sum(stats[3, at, :] * jnp.exp(peak - top), axis=1, keepdims=True)
        column = jnp.broadcast_to(top + jnp.log(total), (LANES, LANES))
        lse[r // LANES : r // LANES + 1, :] = jnp.transpose(column)[:1]
    for t in range(n):
        give(t).wait()


def finish_kernel(k_all, every, score, out, held, done, shift, in_sems, out_sems):
    rows, k_dev = out.shape
    n = in_sems.shape[0]
    block = rows // n

    def bring(t):
        part = pl.ds(t * block, block)
        return pltpu.make_async_copy(score.at[part, :], held.at[part, :], in_sems.at[t])

    def give(t):
        part = pl.ds(t * block, block)
        return pltpu.make_async_copy(done.at[part, :], out.at[part, :], out_sems.at[t])

    bring(0).start()
    bring(1).start()
    for r in range(every.shape[1]):
        each = every[:, r]
        peak = jnp.max(each, axis=0, keepdims=True)
        total = jnp.sum(jnp.exp(each - peak), axis=0, keepdims=True)
        row = peak + jnp.log(total) - jnp.log(jnp.full((1, LANES), k_all, F32))
        shift[r * LANES : (r + 1) * LANES, :] = jnp.transpose(jnp.broadcast_to(row, (LANES, LANES)))
    for t in range(n):
        bring(t).wait()
        if t + 2 < n:
            bring(t + 2).start()

        def group(g, carry):
            at = pl.ds(pl.multiple_of(t * block + g * 16, 16), 16)
            less = shift[at, :]
            for j in range(0, k_dev, LANES):
                done[at, j : j + LANES] = (held[at, j : j + LANES] - less).astype(BF16)
            return carry

        lax.fori_loop(0, block // 16, group, 0)
        give(t).start()
    for t in range(n):
        give(t).wait()


def collect(core, offset, ids, cent):
    rows = ids.shape[0] * MINE
    k_dev, dim = cent.shape
    part = jax.ShapeDtypeStruct((HALF, dim), BF16)
    return pl.pallas_call(
        collect_kernel,
        out_shape=(part, part, jax.ShapeDtypeStruct((rows, LANES), I32), jax.ShapeDtypeStruct((1,), I32)),
        in_specs=[IN_SMEM, IN_SMEM, IN_VMEM, IN_PLACE],
        out_specs=(IN_VMEM, IN_VMEM, IN_VMEM, IN_SMEM),
        scratch_shapes=[
            pltpu.VMEM((SLOTS, dim), F32),
            pltpu.VMEM((SLOTS, 16, dim), BF16),
            pltpu.SMEM((2 * SLOTS,), I32),
            pltpu.SMEM((2 * SLOTS,), I32),
            pltpu.SemaphoreType.DMA((SLOTS,)),
        ],
        compiler_params=PARAMS,
        name="collect",
    )(jnp.stack([core, offset, offset - core * k_dev]).astype(I32), ids, ids, cent)


def scores(pooled, core, own, other, hint, norms, cent):
    chips, _, dim = own.shape
    rows = 2 * chips * MINE
    k_dev = cent.shape[0]
    n = k_dev // STEP
    return pl.pallas_call(
        functools.partial(score_kernel, pooled),
        out_shape=(
            jax.ShapeDtypeStruct((rows, k_dev), F32),
            jax.ShapeDtypeStruct((rows // LANES, LANES), F32),
        ),
        in_specs=[IN_SMEM] + [IN_VMEM] * 4 + [IN_PLACE],
        out_specs=(IN_PLACE, IN_VMEM),
        scratch_shapes=[
            pltpu.VMEM((2 * chips * HALF, dim), BF16),
            pltpu.VMEM((rows, dim), F32),
            pltpu.VMEM((2 * rows, dim), BF16),
            pltpu.VMEM((k_dev, dim), BF16),
            pltpu.VMEM((rows, k_dev), F32),
            pltpu.VMEM((2 * rows, STEP), F32),
            pltpu.VMEM((2 * rows, STEP), F32),
            pltpu.VMEM((4, rows, LANES), F32),
            pltpu.SemaphoreType.DMA((n,)),
            pltpu.SemaphoreType.DMA((n,)),
        ],
        compiler_params=PARAMS,
        name="score",
    )(core.reshape(1).astype(I32), own, other, hint, norms, cent)


def finish(k_all, every, score):
    rows, k_dev = score.shape
    n = 8
    return pl.pallas_call(
        functools.partial(finish_kernel, k_all),
        out_shape=jax.ShapeDtypeStruct((rows, k_dev), BF16),
        in_specs=[IN_VMEM, IN_PLACE],
        out_specs=IN_PLACE,
        scratch_shapes=[
            pltpu.VMEM((rows, k_dev), F32),
            pltpu.VMEM((rows, k_dev), BF16),
            pltpu.VMEM((rows, LANES), F32),
            pltpu.SemaphoreType.DMA((n,)),
            pltpu.SemaphoreType.DMA((n,)),
        ],
        compiler_params=PARAMS,
        name="finish",
    )(every, score)


def send_to_all(block, axes):
    n = lax.axis_size(axes)
    return lax.all_to_all(jnp.broadcast_to(block[None], (n,) + block.shape), axes, 0, 0, tiled=True)


def primaries(core, offset, ids, cent):
    k_dev, dim = cent.shape
    chips = lax.axis_size(CHIPS)
    local = ids[:, 0, :MINE].reshape(chips, 2, MINE) - offset
    local = jnp.where(core == 0, local, local[:, ::-1])
    local = jnp.swapaxes(local, 0, 1).reshape(-1, 1)
    hot = (local == lax.broadcasted_iota(I32, (1, k_dev), 1)).astype(BF16)
    found = jnp.dot(hot, cent, preferred_element_type=F32).astype(BF16).reshape(2, chips, MINE, dim)
    for_me = found[0] + lax.ppermute(found[1], "core", SWAP)
    parts = lax.all_to_all(for_me, CHIPS, 0, 0, tiled=True)
    mine = jnp.sum(parts.astype(F32), axis=0).astype(BF16)
    own = send_to_all(mine, CHIPS)
    other = lax.ppermute(own, "core", SWAP)
    pair = jnp.stack([jnp.where(core == 0, own, other), jnp.where(core == 0, other, own)], axis=1)
    return pair.reshape(-1, dim)


def body(vectors, primary, centroids):
    k_dev, dim = centroids.shape
    owners = lax.axis_size(CENT)
    core = lax.axis_index("core")
    offset = lax.axis_index(CENT) * k_dev

    ids = send_to_all(jnp.pad(primary, (0, LANES - MINE)).reshape(1, LANES), CENT)
    norms = jnp.einsum("kd,kd->k", centroids, centroids, preferred_element_type=F32).reshape(1, k_dev) / 32.0

    keep, away, place, most = collect(core, offset, ids, centroids)
    slots = keep + lax.ppermute(away, "core", SWAP)
    along_z = send_to_all(jnp.concatenate([slots, vectors], axis=0), "z")
    own = send_to_all(along_z, "x").reshape(-1, HALF + MINE, dim)
    other = lax.ppermute(own, "core", SWAP)
    score, lse = lax.cond(
        most[0] < SLOTS,
        lambda: scores(True, core, own, other, place, norms, centroids),
        lambda: scores(False, core, own, other, primaries(core, offset, ids, centroids), norms, centroids),
    )
    every = send_to_all(lse, CENT)
    return finish(k_dev * owners, every, score)


def solution(mesh):
    fine = Mesh(mesh.devices.reshape(4, 8, 2, 4), CENT + ("slab",))
    return jax.shard_map(
        body,
        mesh=fine,
        in_specs=(P(("slab",) + CENT, None), P(("slab",) + CENT), P(CENT, None)),
        out_specs=P("slab", CENT),
        check_vma=False,
    )
```

```python
import functools

import jax
import jax.numpy as jnp
from jax import lax
from jax.experimental import pallas as pl
from jax.experimental.pallas import tpu as pltpu
from jax.sharding import Mesh, PartitionSpec as P

CENT = ("x", "z", "core")
CHIPS = ("x", "z")
SWAP = [(0, 1), (1, 0)]
F32 = jnp.float32
BF16 = jnp.bfloat16
I32 = jnp.int32
IN_VMEM = pl.BlockSpec(memory_space=pltpu.VMEM)
IN_SMEM = pl.BlockSpec(memory_space=pltpu.SMEM)
IN_PLACE = pl.BlockSpec(memory_space=pl.ANY)
PARAMS = pltpu.CompilerParams(vmem_limit_bytes=60 * 1024 * 1024)
SMALL = pltpu.CompilerParams(vmem_limit_bytes=24 * 1024 * 1024)
LANES = 128
X = 4
MINE = 8
STEP = 512
HALF = 16
SLOTS = 2 * HALF


def dot_t(a, b):
    return lax.dot_general(a, b, (((1,), (1,)), ((), ())), preferred_element_type=F32)


def collect_kernel(where, ids, cent, keep, away, place, most, found, stage, named, named_too, sems, sem):
    k_dev, dim = cent.shape
    rows = place.shape[0]
    owners = rows // MINE
    core = where[0]

    row = lax.broadcasted_iota(I32, (owners, MINE, LANES), 1)
    lane = lax.broadcasted_iota(I32, (owners, MINE, LANES), 2)
    each = jnp.broadcast_to(ids[...].astype(F32), (owners, MINE, LANES))
    column = jnp.sum(jnp.where(row == lane, each, 0.0), axis=2, keepdims=True).reshape(rows, 1)
    column = jnp.broadcast_to(column, (rows, LANES))
    chip = jnp.floor(column * (0.5 / k_dev))
    rank = jnp.zeros((rows, LANES), F32)
    before = lax.broadcasted_iota(I32, (rows, LANES), 0)
    after = lax.broadcasted_iota(I32, (rows, LANES), 1)
    for r in range(0, rows, LANES):
        across = jnp.transpose(chip[r : r + LANES])[:1]
        rank = rank + jnp.where((chip == across) & (after + r < before), 1.0, 0.0)
    rank = jnp.broadcast_to(jnp.sum(rank, axis=1, keepdims=True).astype(I32), (rows, LANES))
    here = (rank == after) & (chip.astype(I32) == where[3])
    slot = jnp.sum(jnp.where(here, column + 1.0, 0.0), axis=0, keepdims=True).astype(I32) - 1
    named[...] = jnp.broadcast_to(slot, named.shape)
    tell = pltpu.make_async_copy(named, named_too, sem)
    tell.start()

    half = lax.shift_right_logical(rank, 4) ^ core
    spot = chip.astype(I32)
    spot = ((lax.shift_right_logical(spot, 3) - where[1]) & 3) * 8 + (spot & 7)
    at = half * (rows // (2 * MINE) * HALF) + spot * HALF + (rank & (HALF - 1))
    for r in range(X):
        to = pl.multiple_of(((r - where[1]) & (X - 1)) * LANES, LANES)
        place[pl.ds(to, LANES), :] = at[r * LANES : (r + 1) * LANES]
    most[0] = jnp.max(rank)
    found[...] = jnp.zeros_like(found)
    tell.wait()

    def is_mine(s):
        local = named_too[0, s] - where[2]
        return (local >= 0) & (local < k_dev)

    def bring(s):
        group = pl.multiple_of((named_too[0, s] - where[2]) // 16 * 16, 16)
        return pltpu.make_async_copy(cent.at[pl.ds(group, 16), :], stage.at[s], sems.at[s])

    def start(s, carry):
        @pl.when(is_mine(s))
        def _():
            bring(s).start()

        return carry

    def take(s, carry):
        @pl.when(is_mine(s))
        def _():
            bring(s).wait()
            row = lax.broadcasted_iota(I32, (16, dim), 0)
            inside = lax.rem(named_too[0, s] - where[2], 16)
            picked = jnp.where(row == inside, stage[s].astype(F32), 0.0)
            found[pl.ds(s, 1), :] = jnp.sum(picked, axis=0, keepdims=True)

        return carry

    lax.fori_loop(0, SLOTS, start, 0)
    lax.fori_loop(0, SLOTS, take, 0)
    keep[...] = found[pl.ds(pl.multiple_of(core * HALF, HALF), HALF), :].astype(BF16)
    away[...] = found[pl.ds(pl.multiple_of((1 - core) * HALF, HALF), HALF), :].astype(BF16)


def norms_kernel(cent, norms):
    for r in range(0, cent.shape[0], LANES):
        wide = cent[r : r + LANES, :].astype(F32)
        column = jnp.sum(wide * wide, axis=1, keepdims=True) * (1.0 / 32.0)
        norms[:, r : r + LANES] = jnp.transpose(jnp.broadcast_to(column, (LANES, LANES)))[:1]


def score_kernel(pooled, where, *refs):
    own, other = refs[:5], refs[5:10]
    hint, norms, cent, score, lse, pool, rows_of, both, table, made, held_a, held_b, stats, in_sems, out_sems = refs[10:]
    dim = cent.shape[1]
    chips = sum(ref.shape[0] for ref in own)
    rows = 2 * chips * MINE
    k_dev = cent.shape[0]
    n = k_dev // STEP
    core = where[0]

    def bring(t):
        part = pl.ds(pl.multiple_of(t * STEP, STEP), STEP)
        return pltpu.make_async_copy(cent.at[part, :], table.at[part, :], in_sems.at[t])

    def give(t, r):
        part = pl.ds(pl.multiple_of(t * STEP, STEP), STEP)
        to = pl.ds(pl.multiple_of(((where[1] + r) & (X - 1)) * LANES, LANES), LANES)
        return pltpu.make_async_copy(
            made.at[r * LANES : (r + 1) * LANES, part], score.at[to, part], out_sems.at[t * X + r]
        )

    def give_all(t):
        for r in range(X):
            give(t, r).start()

    bring(0).start()
    bring(1).start()
    if pooled:
        spot = 0
        for ref in (*own, *other):
            for z in range(ref.shape[0]):
                pool[spot : spot + HALF, :] = ref[z, :HALF, :]
                spot += HALF
        lane = lax.broadcasted_iota(I32, (rows, LANES), 1)
        hot = [(hint[...] == lane + j).astype(F32).astype(BF16) for j in range(0, 2 * chips * HALF, LANES)]
        rows_of[...] = jnp.dot(jnp.concatenate(hot, axis=1), pool[...], preferred_element_type=F32)

    first = 0
    for mine, theirs in zip(own, other, strict=True):

        def prepare(z, carry, mine=mine, theirs=theirs, first=first):
            at = pl.ds(pl.multiple_of((first + z) * 2 * MINE, 2 * MINE), 2 * MINE)
            low = pl.ds(pl.multiple_of(rows + (first + z) * 2 * MINE, 2 * MINE), 2 * MINE)
            a = mine[z, HALF : HALF + MINE, :].astype(F32)
            b = theirs[z, HALF : HALF + MINE, :].astype(F32)
            vec = jnp.concatenate([jnp.where(core == 0, a, b), jnp.where(core == 0, b, a)], axis=0)
            near = rows_of[at, :] if pooled else hint[at, :].astype(F32)
            rounded = (vec - near).astype(BF16)
            res = rounded.astype(F32)
            both[at, :] = vec.astype(BF16)
            both[low, :] = rounded
            along = jnp.sum(vec * res, axis=1, keepdims=True)
            energy = 1e-06 + jnp.sum(res * res, axis=1, keepdims=True)
            stats[0, at, :] = jnp.broadcast_to(along, (2 * MINE, LANES))
            stats[1, at, :] = jnp.broadcast_to((1.0 / 32.0) / energy, (2 * MINE, LANES))
            return carry

        lax.fori_loop(0, mine.shape[0], prepare, 0, unroll=4)
        first += mine.shape[0]
    stats[2] = jnp.full((rows, LANES), -jnp.inf, F32)
    stats[3] = jnp.zeros((rows, LANES), F32)
    held_b[...] = jnp.full_like(held_b, -1e30)
    held_b[rows:, :] = jnp.zeros((rows, STEP), F32)

    def product(held, t):
        part = pl.ds(pl.multiple_of(t * STEP, STEP), STEP)
        held[...] = dot_t(both[...], table[part, :])

    def settle(held, t):
        first = pl.multiple_of(t * STEP, STEP)
        for g in range(0, rows, 8):
            at, low = slice(g, g + 8), slice(rows + g, rows + g + 8)
            along, weight, peak = stats[0, at, :], stats[1, at, :], stats[2, at, :]
            parts = []
            for j in range(0, STEP, LANES):
                cols = pl.ds(first + j, LANES)
                gap = along - held[low, j : j + LANES]
                part = held[at, j : j + LANES] * (1.0 / 16.0) - norms[:, cols] - gap * gap * weight
                made[at, cols] = part
                parts.append(part)
            new = functools.reduce(jnp.maximum, parts, peak)
            sums = [jnp.exp(part - new) for part in parts]
            while len(sums) > 1:
                sums = [sums[i] + sums[i + 1] for i in range(0, len(sums), 2)]
            stats[3, at, :] = stats[3, at, :] * jnp.exp(peak - new) + sums[0]
            stats[2, at, :] = new

    def turn(i, carry):
        bring(2 * i).wait()
        bring(2 * i + 1).wait()

        @pl.when(i + 1 < n // 2)
        def _():
            bring(2 * i + 2).start()
            bring(2 * i + 3).start()

        product(held_a, 2 * i)
        settle(held_b, jnp.maximum(2 * i - 1, 0))
        product(held_b, 2 * i + 1)
        settle(held_a, 2 * i)

        @pl.when(i > 0)
        def _():
            give_all(2 * i - 1)

        give_all(2 * i)
        return carry

    lax.fori_loop(0, n // 2, turn, 0)
    settle(held_b, n - 1)
    give_all(n - 1)
    for r in range(X):
        at = slice(r * LANES, (r + 1) * LANES)
        peak = stats[2, at, :]
        top = jnp.max(peak, axis=1, keepdims=True)
        total = jnp.sum(stats[3, at, :] * jnp.exp(peak - top), axis=1, keepdims=True)
        column = jnp.broadcast_to(top + jnp.log(total), (LANES, LANES))
        lse[pl.ds((where[1] + r) & (X - 1), 1), :] = jnp.transpose(column)[:1]
    for t in range(n):
        for r in range(X):
            give(t, r).wait()


def finish_kernel(k_all, every, held, out, done, shift, sems):
    rows, k_dev = out.shape
    n = sems.shape[0]
    block = rows // n

    def give(t):
        part = pl.ds(t * block, block)
        return pltpu.make_async_copy(done.at[part, :], out.at[part, :], sems.at[t])

    for r in range(every.shape[1]):
        each = every[:, r]
        peak = jnp.max(each, axis=0, keepdims=True)
        total = jnp.sum(jnp.exp(each - peak), axis=0, keepdims=True)
        row = peak + jnp.log(total) - jnp.log(jnp.full((1, LANES), k_all, F32))
        shift[r * LANES : (r + 1) * LANES, :] = jnp.transpose(jnp.broadcast_to(row, (LANES, LANES)))
    for t in range(n):

        def group(g, carry):
            at = pl.ds(pl.multiple_of(t * block + g * 16, 16), 16)
            less = shift[at, :]
            for j in range(0, k_dev, LANES):
                done[at, j : j + LANES] = (held[at, j : j + LANES] - less).astype(BF16)
            return carry

        lax.fori_loop(0, block // 16, group, 0)
        give(t).start()
    for t in range(n):
        give(t).wait()


def collect(where, ids, cent):
    rows = ids.shape[0] * MINE
    k_dev, dim = cent.shape
    part = jax.ShapeDtypeStruct((HALF, dim), BF16)
    return pl.pallas_call(
        collect_kernel,
        out_shape=(part, part, jax.ShapeDtypeStruct((rows, LANES), I32), jax.ShapeDtypeStruct((1,), I32)),
        in_specs=[IN_SMEM, IN_VMEM, IN_PLACE],
        out_specs=(IN_VMEM, IN_VMEM, IN_VMEM, IN_SMEM),
        scratch_shapes=[
            pltpu.VMEM((SLOTS, dim), F32),
            pltpu.VMEM((SLOTS, 16, dim), BF16),
            pltpu.VMEM((8, LANES), I32),
            pltpu.SMEM((8, LANES), I32),
            pltpu.SemaphoreType.DMA((SLOTS,)),
            pltpu.SemaphoreType.DMA,
        ],
        compiler_params=PARAMS,
        name="collect",
    )(where, ids, cent)


def norms_of(cent):
    k_dev, dim = cent.shape
    return pl.pallas_call(
        norms_kernel,
        grid=(4,),
        out_shape=jax.ShapeDtypeStruct((1, k_dev), F32),
        in_specs=[pl.BlockSpec((k_dev // 4, dim), lambda i: (i, 0))],
        out_specs=pl.BlockSpec((1, k_dev // 4), lambda i: (0, i)),
        compiler_params=PARAMS,
        cost_estimate=pl.CostEstimate(flops=4 * cent.size, bytes_accessed=2 * cent.size, transcendentals=0),
        name="norms",
    )(cent)


def scores(pooled, where, blocks, hint, norms, cent):
    k_dev, dim = cent.shape
    rows = hint.shape[0]
    chips = rows // (2 * MINE)
    n = k_dev // STEP
    return pl.pallas_call(
        functools.partial(score_kernel, pooled),
        out_shape=(
            jax.ShapeDtypeStruct((rows, k_dev), F32),
            jax.ShapeDtypeStruct((X, LANES), F32),
        ),
        in_specs=[IN_SMEM] + [IN_VMEM] * (len(blocks) + 2) + [IN_PLACE],
        out_specs=(IN_PLACE, IN_VMEM),
        scratch_shapes=[
            pltpu.VMEM((2 * chips * HALF, dim), BF16),
            pltpu.VMEM((rows, dim), F32),
            pltpu.VMEM((2 * rows, dim), BF16),
            pltpu.VMEM((k_dev, dim), BF16),
            pltpu.VMEM((rows, k_dev), F32),
            pltpu.VMEM((2 * rows, STEP), F32),
            pltpu.VMEM((2 * rows, STEP), F32),
            pltpu.VMEM((4, rows, LANES), F32),
            pltpu.SemaphoreType.DMA((n,)),
            pltpu.SemaphoreType.DMA((n * X,)),
        ],
        compiler_params=PARAMS,
        name="score",
    )(where, *blocks, hint, norms, cent)


def finish(k_all, every, held):
    rows, k_dev = held.shape
    n = 8
    return pl.pallas_call(
        functools.partial(finish_kernel, k_all),
        out_shape=jax.ShapeDtypeStruct((rows, k_dev), BF16),
        in_specs=[IN_VMEM, IN_VMEM],
        out_specs=IN_PLACE,
        scratch_shapes=[
            pltpu.VMEM((rows, k_dev), BF16),
            pltpu.VMEM((rows, LANES), F32),
            pltpu.SemaphoreType.DMA((n,)),
        ],
        compiler_params=SMALL,
        name="finish",
    )(every, pltpu.with_memory_space_constraint(held, pltpu.VMEM))


def send_to_all(block, axes):
    n = lax.axis_size(axes)
    return lax.all_to_all(jnp.broadcast_to(block[None], (n,) + block.shape), axes, 0, 0, tiled=True)


def primaries(core, offset, ids, cent):
    k_dev, dim = cent.shape
    chips = lax.axis_size(CHIPS)
    local = ids[:, 0, :MINE].reshape(chips, 2, MINE) - offset
    local = jnp.where(core == 0, local, local[:, ::-1])
    local = jnp.swapaxes(local, 0, 1).reshape(-1, 1)
    hot = (local == lax.broadcasted_iota(I32, (1, k_dev), 1)).astype(BF16)
    found = jnp.dot(hot, cent, preferred_element_type=F32).astype(BF16).reshape(2, chips, MINE, dim)
    for_me = found[0] + lax.ppermute(found[1], "core", SWAP)
    parts = lax.all_to_all(for_me, CHIPS, 0, 0, tiled=True)
    mine = jnp.sum(parts.astype(F32), axis=0).astype(BF16)
    own = send_to_all(mine, CHIPS)
    other = lax.ppermute(own, "core", SWAP)
    pair = jnp.stack([jnp.where(core == 0, own, other), jnp.where(core == 0, other, own)], axis=1)
    return pair.reshape(-1, dim)


def body(vectors, primary, centroids):
    k_dev, dim = centroids.shape
    owners = lax.axis_size(CENT)
    core, x = lax.axis_index("core"), lax.axis_index("x")
    offset = lax.axis_index(CENT) * k_dev
    where = jnp.stack([core, x, offset, lax.axis_index(CHIPS)]).astype(I32)

    ids = send_to_all(jnp.pad(primary, (0, LANES - MINE)).reshape(1, LANES), CENT)
    norms = norms_of(centroids)

    keep, away, place, most = collect(where, ids, centroids)
    slots = keep + lax.ppermute(away, "core", SWAP)
    column = send_to_all(jnp.concatenate([slots, vectors], axis=0), "z")
    after = lax.ppermute(column, "x", [(i, (i - 1) % X) for i in range(X)])
    before = lax.ppermute(column, "x", [(i, (i + 1) % X) for i in range(X)])
    middle = column.shape[0] // 2
    one, two, norms = lax.optimization_barrier((before[:middle], after[middle:], norms))
    far = (
        lax.ppermute(one, "x", [(i, (i + 1) % X) for i in range(X)]),
        lax.ppermute(two, "x", [(i, (i - 1) % X) for i in range(X)]),
    )
    own = (column, after, *far, before)
    blocks = (*own, *(lax.ppermute(block, "core", SWAP) for block in own))

    def dense():
        near = primaries(core, offset, ids, centroids).reshape(X, -1, dim)
        near = jnp.take(near, (x + jnp.arange(X)) % X, axis=0).reshape(-1, dim)
        return scores(False, where, blocks, near, norms, centroids)

    score, lse = lax.cond(
        most[0] < SLOTS, lambda: scores(True, where, blocks, place, norms, centroids), dense
    )
    every = send_to_all(lse, CENT)
    return finish(k_dev * owners, every, score)


def solution(mesh):
    fine = Mesh(mesh.devices.reshape(4, 8, 2, 4), CENT + ("slab",))
    return jax.shard_map(
        body,
        mesh=fine,
        in_specs=(P(("slab",) + CENT, None), P(("slab",) + CENT), P(CENT, None)),
        out_specs=P("slab", CENT),
        check_vma=False,
    )
```

```python
import functools

import jax
import jax.numpy as jnp
from jax import lax
from jax.experimental import pallas as pl
from jax.experimental.pallas import tpu as pltpu
from jax.sharding import Mesh, PartitionSpec as P

CENT = ("x", "z", "core")
CHIPS = ("x", "z")
SWAP = [(0, 1), (1, 0)]
F32 = jnp.float32
BF16 = jnp.bfloat16
I32 = jnp.int32
IN_VMEM = pl.BlockSpec(memory_space=pltpu.VMEM)
IN_SMEM = pl.BlockSpec(memory_space=pltpu.SMEM)
IN_PLACE = pl.BlockSpec(memory_space=pl.ANY)
PARAMS = pltpu.CompilerParams(vmem_limit_bytes=60 * 1024 * 1024)
SMALL = pltpu.CompilerParams(vmem_limit_bytes=24 * 1024 * 1024)
LANES = 128
X = 4
MINE = 8
STEP = 512
HALF = 16
SLOTS = 2 * HALF


def dot_t(a, b):
    return lax.dot_general(a, b, (((1,), (1,)), ((), ())), preferred_element_type=F32)


def collect_kernel(where, ids, cent, keep, away, place, most, found, stage, named, named_too, sems, sem):
    k_dev, dim = cent.shape
    rows = place.shape[0]
    owners = rows // MINE
    core = where[0]

    row = lax.broadcasted_iota(I32, (owners, MINE, MINE), 1)
    lane = lax.broadcasted_iota(I32, (owners, MINE, MINE), 2)
    each = jnp.broadcast_to(ids[...].astype(F32), (owners, MINE, MINE))
    column = jnp.sum(jnp.where(row == lane, each, 0.0), axis=2, keepdims=True).reshape(rows, 1)
    column = jnp.broadcast_to(column, (rows, LANES))
    chip = jnp.floor(column * (0.5 / k_dev))
    rank = jnp.zeros((rows, LANES), F32)
    before = lax.broadcasted_iota(I32, (rows, LANES), 0)
    after = lax.broadcasted_iota(I32, (rows, LANES), 1)
    for r in range(0, rows, LANES):
        across = jnp.transpose(chip[r : r + LANES])[:1]
        rank = rank + jnp.where((chip == across) & (after + r < before), 1.0, 0.0)
    rank = jnp.broadcast_to(jnp.sum(rank, axis=1, keepdims=True).astype(I32), (rows, LANES))
    here = (rank == after) & (chip.astype(I32) == where[3])
    slot = jnp.sum(jnp.where(here, column + 1.0, 0.0), axis=0, keepdims=True).astype(I32) - 1
    named[...] = jnp.broadcast_to(slot, named.shape)
    tell = pltpu.make_async_copy(named, named_too, sem)
    tell.start()

    half = lax.shift_right_logical(rank, 4) ^ core
    spot = chip.astype(I32)
    spot = ((lax.shift_right_logical(spot, 3) - where[1]) & 3) * 8 + (spot & 7)
    at = half * (rows // (2 * MINE) * HALF) + spot * HALF + (rank & (HALF - 1))
    for r in range(X):
        to = pl.multiple_of(((r - where[1]) & (X - 1)) * LANES, LANES)
        place[pl.ds(to, LANES), :] = at[r * LANES : (r + 1) * LANES]
    most[0] = jnp.max(rank)
    found[...] = jnp.zeros_like(found)
    tell.wait()

    def is_mine(s):
        local = named_too[0, s] - where[2]
        return (local >= 0) & (local < k_dev)

    def bring(s):
        group = pl.multiple_of((named_too[0, s] - where[2]) // 16 * 16, 16)
        return pltpu.make_async_copy(cent.at[pl.ds(group, 16), :], stage.at[s], sems.at[s])

    def start(s, carry):
        @pl.when(is_mine(s))
        def _():
            bring(s).start()

        return carry

    def take(s, carry):
        @pl.when(is_mine(s))
        def _():
            bring(s).wait()
            row = lax.broadcasted_iota(I32, (16, dim), 0)
            inside = lax.rem(named_too[0, s] - where[2], 16)
            picked = jnp.where(row == inside, stage[s].astype(F32), 0.0)
            found[pl.ds(s, 1), :] = jnp.sum(picked, axis=0, keepdims=True)

        return carry

    lax.fori_loop(0, SLOTS, start, 0)
    lax.fori_loop(0, SLOTS, take, 0)
    keep[...] = found[pl.ds(pl.multiple_of(core * HALF, HALF), HALF), :].astype(BF16)
    away[...] = found[pl.ds(pl.multiple_of((1 - core) * HALF, HALF), HALF), :].astype(BF16)


def norms_kernel(cent, norms):
    for r in range(0, cent.shape[0], LANES):
        wide = cent[r : r + LANES, :].astype(F32)
        column = jnp.sum(wide * wide, axis=1, keepdims=True) * (1.0 / 32.0)
        norms[:, r : r + LANES] = jnp.transpose(jnp.broadcast_to(column, (LANES, LANES)))[:1]


def score_kernel(pooled, where, *refs):
    own, other = refs[:8], refs[8:16]
    hint, norms, cent, score, lse, pool, rows_of, both, table, made, held_a, held_b, stats, in_sems, out_sems = refs[16:]
    dim = cent.shape[1]
    chips = sum(ref.shape[0] for ref in own)
    rows = 2 * chips * MINE
    k_dev = cent.shape[0]
    n = k_dev // STEP
    core = where[0]

    def bring(t):
        part = pl.ds(pl.multiple_of(t * STEP, STEP), STEP)
        return pltpu.make_async_copy(cent.at[part, :], table.at[part, :], in_sems.at[t])

    def give(t, r):
        part = pl.ds(pl.multiple_of(t * STEP, STEP), STEP)
        to = pl.ds(pl.multiple_of(((where[1] + r) & (X - 1)) * LANES, LANES), LANES)
        return pltpu.make_async_copy(
            made.at[r * LANES : (r + 1) * LANES, part], score.at[to, part], out_sems.at[t * X + r]
        )

    def give_all(t):
        for r in range(X):
            give(t, r).start()

    bring(0).start()
    bring(1).start()
    if pooled:
        spot = 0
        for ref in (*own, *other):
            for z in range(ref.shape[0]):
                pool[spot : spot + HALF, :] = ref[z, :HALF, :]
                spot += HALF
        lane = lax.broadcasted_iota(I32, (rows, LANES), 1)
        hot = [(hint[...] == lane + j).astype(F32).astype(BF16) for j in range(0, 2 * chips * HALF, LANES)]
        rows_of[...] = jnp.dot(jnp.concatenate(hot, axis=1), pool[...], preferred_element_type=F32)

    first = 0
    for mine, theirs in zip(own, other, strict=True):

        def prepare(z, carry, mine=mine, theirs=theirs, first=first):
            at = pl.ds(pl.multiple_of((first + z) * 2 * MINE, 2 * MINE), 2 * MINE)
            low = pl.ds(pl.multiple_of(rows + (first + z) * 2 * MINE, 2 * MINE), 2 * MINE)
            a = mine[z, HALF : HALF + MINE, :].astype(F32)
            b = theirs[z, HALF : HALF + MINE, :].astype(F32)
            vec = jnp.concatenate([jnp.where(core == 0, a, b), jnp.where(core == 0, b, a)], axis=0)
            near = rows_of[at, :] if pooled else hint[at, :].astype(F32)
            rounded = (vec - near).astype(BF16)
            res = rounded.astype(F32)
            both[at, :] = vec.astype(BF16)
            both[low, :] = rounded
            along = jnp.sum(vec * res, axis=1, keepdims=True)
            energy = 1e-06 + jnp.sum(res * res, axis=1, keepdims=True)
            stats[0, at, :] = jnp.broadcast_to(along, (2 * MINE, LANES))
            stats[1, at, :] = jnp.broadcast_to((1.0 / 32.0) / energy, (2 * MINE, LANES))
            return carry

        lax.fori_loop(0, mine.shape[0], prepare, 0, unroll=4)
        first += mine.shape[0]
    stats[2] = jnp.full((rows, LANES), -jnp.inf, F32)
    stats[3] = jnp.zeros((rows, LANES), F32)
    held_b[...] = jnp.full_like(held_b, -1e30)
    held_b[rows:, :] = jnp.zeros((rows, STEP), F32)

    def product(held, t):
        part = pl.ds(pl.multiple_of(t * STEP, STEP), STEP)
        held[...] = dot_t(both[...], table[part, :])

    def settle(held, t):
        first = pl.multiple_of(t * STEP, STEP)
        for g in range(0, rows, 8):
            at, low = slice(g, g + 8), slice(rows + g, rows + g + 8)
            along, weight, peak = stats[0, at, :], stats[1, at, :], stats[2, at, :]
            parts = []
            for j in range(0, STEP, LANES):
                cols = pl.ds(first + j, LANES)
                gap = along - held[low, j : j + LANES]
                part = held[at, j : j + LANES] * (1.0 / 16.0) - norms[:, cols] - gap * gap * weight
                made[at, cols] = part
                parts.append(part)
            new = functools.reduce(jnp.maximum, parts, peak)
            sums = [jnp.exp(part - new) for part in parts]
            while len(sums) > 1:
                sums = [sums[i] + sums[i + 1] for i in range(0, len(sums), 2)]
            stats[3, at, :] = stats[3, at, :] * jnp.exp(peak - new) + sums[0]
            stats[2, at, :] = new

    def turn(i, carry):
        bring(2 * i).wait()
        bring(2 * i + 1).wait()

        @pl.when(i + 1 < n // 2)
        def _():
            bring(2 * i + 2).start()
            bring(2 * i + 3).start()

        product(held_a, 2 * i)
        settle(held_b, jnp.maximum(2 * i - 1, 0))
        product(held_b, 2 * i + 1)
        settle(held_a, 2 * i)

        @pl.when(i > 0)
        def _():
            give_all(2 * i - 1)

        give_all(2 * i)
        return carry

    lax.fori_loop(0, n // 2, turn, 0)
    settle(held_b, n - 1)
    give_all(n - 1)
    for r in range(X):
        at = slice(r * LANES, (r + 1) * LANES)
        peak = stats[2, at, :]
        top = jnp.max(peak, axis=1, keepdims=True)
        total = jnp.sum(stats[3, at, :] * jnp.exp(peak - top), axis=1, keepdims=True)
        column = jnp.broadcast_to(top + jnp.log(total), (LANES, LANES))
        lse[pl.ds((where[1] + r) & (X - 1), 1), :] = jnp.transpose(column)[:1]
    for t in range(n):
        for r in range(X):
            give(t, r).wait()


def finish_kernel(k_all, every, held, out, done, shift, sems):
    rows, k_dev = out.shape
    n = sems.shape[0]
    block = rows // n

    def give(t):
        part = pl.ds(t * block, block)
        return pltpu.make_async_copy(done.at[part, :], out.at[part, :], sems.at[t])

    for r in range(every.shape[1]):
        each = every[:, r]
        peak = jnp.max(each, axis=0, keepdims=True)
        total = jnp.sum(jnp.exp(each - peak), axis=0, keepdims=True)
        row = peak + jnp.log(total) - jnp.log(jnp.full((1, LANES), k_all, F32))
        shift[r * LANES : (r + 1) * LANES, :] = jnp.transpose(jnp.broadcast_to(row, (LANES, LANES)))
    for t in range(n):

        def group(g, carry):
            at = pl.ds(pl.multiple_of(t * block + g * 16, 16), 16)
            less = shift[at, :]
            for j in range(0, k_dev, LANES):
                done[at, j : j + LANES] = (held[at, j : j + LANES] - less).astype(BF16)
            return carry

        lax.fori_loop(0, block // 16, group, 0)
        give(t).start()
    for t in range(n):
        give(t).wait()


def collect(where, ids, cent):
    rows = ids.shape[0] * MINE
    k_dev, dim = cent.shape
    part = jax.ShapeDtypeStruct((HALF, dim), BF16)
    return pl.pallas_call(
        collect_kernel,
        out_shape=(part, part, jax.ShapeDtypeStruct((rows, LANES), I32), jax.ShapeDtypeStruct((1,), I32)),
        in_specs=[IN_SMEM, IN_VMEM, IN_PLACE],
        out_specs=(IN_VMEM, IN_VMEM, IN_VMEM, IN_SMEM),
        scratch_shapes=[
            pltpu.VMEM((SLOTS, dim), F32),
            pltpu.VMEM((SLOTS, 16, dim), BF16),
            pltpu.VMEM((8, LANES), I32),
            pltpu.SMEM((8, LANES), I32),
            pltpu.SemaphoreType.DMA((SLOTS,)),
            pltpu.SemaphoreType.DMA,
        ],
        compiler_params=PARAMS,
        name="collect",
    )(where, ids, cent)


def norms_of(cent):
    k_dev, dim = cent.shape
    return pl.pallas_call(
        norms_kernel,
        grid=(4,),
        out_shape=jax.ShapeDtypeStruct((1, k_dev), F32),
        in_specs=[pl.BlockSpec((k_dev // 4, dim), lambda i: (i, 0))],
        out_specs=pl.BlockSpec((1, k_dev // 4), lambda i: (0, i)),
        compiler_params=PARAMS,
        cost_estimate=pl.CostEstimate(flops=4 * cent.size, bytes_accessed=2 * cent.size, transcendentals=0),
        name="norms",
    )(cent)


def scores(pooled, where, blocks, hint, norms, cent):
    k_dev, dim = cent.shape
    rows = hint.shape[0]
    chips = rows // (2 * MINE)
    n = k_dev // STEP
    return pl.pallas_call(
        functools.partial(score_kernel, pooled),
        out_shape=(
            jax.ShapeDtypeStruct((rows, k_dev), F32),
            jax.ShapeDtypeStruct((X, LANES), F32),
        ),
        in_specs=[IN_SMEM] + [IN_VMEM] * (len(blocks) + 2) + [IN_PLACE],
        out_specs=(IN_PLACE, IN_VMEM),
        scratch_shapes=[
            pltpu.VMEM((2 * chips * HALF, dim), BF16),
            pltpu.VMEM((rows, dim), F32),
            pltpu.VMEM((2 * rows, dim), BF16),
            pltpu.VMEM((k_dev, dim), BF16),
            pltpu.VMEM((rows, k_dev), F32),
            pltpu.VMEM((2 * rows, STEP), F32),
            pltpu.VMEM((2 * rows, STEP), F32),
            pltpu.VMEM((4, rows, LANES), F32),
            pltpu.SemaphoreType.DMA((n,)),
            pltpu.SemaphoreType.DMA((n * X,)),
        ],
        compiler_params=PARAMS,
        name="score",
    )(where, *blocks, hint, norms, cent)


def finish(k_all, every, held):
    rows, k_dev = held.shape
    n = 8
    return pl.pallas_call(
        functools.partial(finish_kernel, k_all),
        out_shape=jax.ShapeDtypeStruct((rows, k_dev), BF16),
        in_specs=[IN_VMEM, IN_VMEM],
        out_specs=IN_PLACE,
        scratch_shapes=[
            pltpu.VMEM((rows, k_dev), BF16),
            pltpu.VMEM((rows, LANES), F32),
            pltpu.SemaphoreType.DMA((n,)),
        ],
        compiler_params=SMALL,
        name="finish",
    )(every, pltpu.with_memory_space_constraint(held, pltpu.VMEM))


def send_to_all(block, axes):
    n = lax.axis_size(axes)
    return lax.all_to_all(jnp.broadcast_to(block[None], (n,) + block.shape), axes, 0, 0, tiled=True)


def primaries(core, offset, ids, cent):
    k_dev, dim = cent.shape
    chips = lax.axis_size(CHIPS)
    local = ids[:, 0].reshape(chips, 2, MINE) - offset
    local = jnp.where(core == 0, local, local[:, ::-1])
    local = jnp.swapaxes(local, 0, 1).reshape(-1, 1)
    hot = (local == lax.broadcasted_iota(I32, (1, k_dev), 1)).astype(BF16)
    found = jnp.dot(hot, cent, preferred_element_type=F32).astype(BF16).reshape(2, chips, MINE, dim)
    for_me = found[0] + lax.ppermute(found[1], "core", SWAP)
    parts = lax.all_to_all(for_me, CHIPS, 0, 0, tiled=True)
    mine = jnp.sum(parts.astype(F32), axis=0).astype(BF16)
    own = send_to_all(mine, CHIPS)
    other = lax.ppermute(own, "core", SWAP)
    pair = jnp.stack([jnp.where(core == 0, own, other), jnp.where(core == 0, other, own)], axis=1)
    return pair.reshape(-1, dim)


def body(vectors, primary, centroids):
    k_dev, dim = centroids.shape
    owners = lax.axis_size(CENT)
    core, x = lax.axis_index("core"), lax.axis_index("x")
    offset = lax.axis_index(CENT) * k_dev
    where = jnp.stack([core, x, offset, lax.axis_index(CHIPS)]).astype(I32)

    ids = send_to_all(primary.reshape(1, MINE), CENT)
    ids, norms = lax.optimization_barrier((ids, norms_of(centroids)))

    keep, away, place, most = collect(where, ids, centroids)
    slots = keep + lax.ppermute(away, "core", SWAP)
    column = send_to_all(jnp.concatenate([slots, vectors], axis=0), "z")
    up = [(i, (i + 1) % X) for i in range(X)]
    down = [(i, (i - 1) % X) for i in range(X)]
    middle = column.shape[0] // 2
    low, high = column[:middle], column[middle:]
    before_low, after_high = lax.ppermute(low, "x", up), lax.ppermute(high, "x", down)
    before_high, after_low = lax.ppermute(high, "x", up), lax.ppermute(low, "x", down)
    far_low, far_high = lax.ppermute(before_low, "x", up), lax.ppermute(after_high, "x", down)
    own = (low, high, after_low, after_high, far_low, far_high, before_low, before_high)
    blocks = (*own, *(lax.ppermute(block, "core", SWAP) for block in own))

    def dense():
        near = primaries(core, offset, ids, centroids).reshape(X, -1, dim)
        near = jnp.take(near, (x + jnp.arange(X)) % X, axis=0).reshape(-1, dim)
        return scores(False, where, blocks, near, norms, centroids)

    score, lse = lax.cond(
        most[0] < SLOTS, lambda: scores(True, where, blocks, place, norms, centroids), dense
    )
    every = send_to_all(lse, CENT)
    return finish(k_dev * owners, every, score)


def solution(mesh):
    fine = Mesh(mesh.devices.reshape(4, 8, 2, 4), CENT + ("slab",))
    return jax.shard_map(
        body,
        mesh=fine,
        in_specs=(P(("slab",) + CENT, None), P(("slab",) + CENT), P(CENT, None)),
        out_specs=P("slab", CENT),
        check_vma=False,
    )
```

```python
import functools

import jax
import jax.numpy as jnp
from jax import lax
from jax.experimental import pallas as pl
from jax.experimental.pallas import tpu as pltpu
from jax.sharding import Mesh, PartitionSpec as P

CENT = ("x", "z", "core")
CHIPS = ("x", "z")
SWAP = [(0, 1), (1, 0)]
F32 = jnp.float32
BF16 = jnp.bfloat16
I32 = jnp.int32
IN_VMEM = pl.BlockSpec(memory_space=pltpu.VMEM)
IN_SMEM = pl.BlockSpec(memory_space=pltpu.SMEM)
IN_PLACE = pl.BlockSpec(memory_space=pl.ANY)
PARAMS = pltpu.CompilerParams(vmem_limit_bytes=60 * 1024 * 1024)
SMALL = pltpu.CompilerParams(vmem_limit_bytes=24 * 1024 * 1024)
LANES = 128
X = 4
MINE = 8
STEP = 512
HALF = 16
SLOTS = 2 * HALF


def dot_t(a, b):
    return lax.dot_general(a, b, (((1,), (1,)), ((), ())), preferred_element_type=F32)


def collect_kernel(where, ids, cent, keep, away, place, most, found, stage, named, named_too, sems, sem):
    k_dev, dim = cent.shape
    rows = place.shape[0]
    owners = rows // MINE
    core = where[0]

    row = lax.broadcasted_iota(I32, (owners, MINE, MINE), 1)
    lane = lax.broadcasted_iota(I32, (owners, MINE, MINE), 2)
    each = jnp.broadcast_to(ids[...].astype(F32), (owners, MINE, MINE))
    column = jnp.sum(jnp.where(row == lane, each, 0.0), axis=2, keepdims=True).reshape(rows, 1)
    column = jnp.broadcast_to(column, (rows, LANES))
    chip = jnp.floor(column * (0.5 / k_dev))
    rank = jnp.zeros((rows, LANES), F32)
    before = lax.broadcasted_iota(I32, (rows, LANES), 0)
    after = lax.broadcasted_iota(I32, (rows, LANES), 1)
    for r in range(0, rows, LANES):
        across = jnp.transpose(chip[r : r + LANES])[:1]
        rank = rank + jnp.where((chip == across) & (after + r < before), 1.0, 0.0)
    rank = jnp.broadcast_to(jnp.sum(rank, axis=1, keepdims=True).astype(I32), (rows, LANES))
    here = (rank == after) & (chip.astype(I32) == where[3])
    slot = jnp.sum(jnp.where(here, column + 1.0, 0.0), axis=0, keepdims=True).astype(I32) - 1
    named[...] = jnp.broadcast_to(slot, named.shape)
    tell = pltpu.make_async_copy(named, named_too, sem)
    tell.start()

    half = lax.shift_right_logical(rank, 4) ^ core
    spot = chip.astype(I32)
    spot = ((lax.shift_right_logical(spot, 3) - where[1]) & 3) * 8 + (spot & 7)
    at = half * (rows // (2 * MINE) * HALF) + spot * HALF + (rank & (HALF - 1))
    for r in range(X):
        to = pl.multiple_of(((r - where[1]) & (X - 1)) * LANES, LANES)
        place[pl.ds(to, LANES), :] = at[r * LANES : (r + 1) * LANES]
    most[0] = jnp.max(rank)
    found[...] = jnp.zeros_like(found)
    tell.wait()

    def is_mine(s):
        local = named_too[0, s] - where[2]
        return (local >= 0) & (local < k_dev)

    def bring(s):
        group = pl.multiple_of((named_too[0, s] - where[2]) // 16 * 16, 16)
        return pltpu.make_async_copy(cent.at[pl.ds(group, 16), :], stage.at[s], sems.at[s])

    def start(s, carry):
        @pl.when(is_mine(s))
        def _():
            bring(s).start()

        return carry

    def take(s, carry):
        @pl.when(is_mine(s))
        def _():
            bring(s).wait()
            row = lax.broadcasted_iota(I32, (16, dim), 0)
            inside = lax.rem(named_too[0, s] - where[2], 16)
            picked = jnp.where(row == inside, stage[s].astype(F32), 0.0)
            found[pl.ds(s, 1), :] = jnp.sum(picked, axis=0, keepdims=True)

        return carry

    lax.fori_loop(0, SLOTS, start, 0)
    lax.fori_loop(0, SLOTS, take, 0)
    keep[...] = found[pl.ds(pl.multiple_of(core * HALF, HALF), HALF), :].astype(BF16)
    away[...] = found[pl.ds(pl.multiple_of((1 - core) * HALF, HALF), HALF), :].astype(BF16)


def norms_kernel(cent, norms):
    for r in range(0, cent.shape[0], LANES):
        wide = cent[r : r + LANES, :].astype(F32)
        column = jnp.sum(wide * wide, axis=1, keepdims=True) * (1.0 / 32.0)
        norms[:, r : r + LANES] = jnp.transpose(jnp.broadcast_to(column, (LANES, LANES)))[:1]


def score_kernel(pooled, where, *refs):
    own, other = refs[:5], refs[5:10]
    hint, norms, cent, score, lse, pool, rows_of, both, table, made, held_a, held_b, stats, in_sems, out_sems = refs[10:]
    dim = cent.shape[1]
    chips = sum(ref.shape[0] for ref in own)
    rows = 2 * chips * MINE
    k_dev = cent.shape[0]
    n = k_dev // STEP
    core = where[0]

    def bring(t):
        part = pl.ds(pl.multiple_of(t * STEP, STEP), STEP)
        return pltpu.make_async_copy(cent.at[part, :], table.at[part, :], in_sems.at[t])

    def give(t, r):
        part = pl.ds(pl.multiple_of(t * STEP, STEP), STEP)
        to = pl.ds(pl.multiple_of(((where[1] + r) & (X - 1)) * LANES, LANES), LANES)
        return pltpu.make_async_copy(
            made.at[r * LANES : (r + 1) * LANES, part], score.at[to, part], out_sems.at[t * X + r]
        )

    def give_all(t):
        for r in range(X):
            give(t, r).start()

    bring(0).start()
    bring(1).start()
    if pooled:
        spot = 0
        for ref in (*own, *other):
            for z in range(ref.shape[0]):
                pool[spot : spot + HALF, :] = ref[z, :HALF, :]
                spot += HALF
        lane = lax.broadcasted_iota(I32, (rows, LANES), 1)
        hot = [(hint[...] == lane + j).astype(F32).astype(BF16) for j in range(0, 2 * chips * HALF, LANES)]
        rows_of[...] = jnp.dot(jnp.concatenate(hot, axis=1), pool[...], preferred_element_type=F32)

    first = 0
    for mine, theirs in zip(own, other, strict=True):

        def prepare(z, carry, mine=mine, theirs=theirs, first=first):
            at = pl.ds(pl.multiple_of((first + z) * 2 * MINE, 2 * MINE), 2 * MINE)
            low = pl.ds(pl.multiple_of(rows + (first + z) * 2 * MINE, 2 * MINE), 2 * MINE)
            a = mine[z, HALF : HALF + MINE, :].astype(F32)
            b = theirs[z, HALF : HALF + MINE, :].astype(F32)
            vec = jnp.concatenate([jnp.where(core == 0, a, b), jnp.where(core == 0, b, a)], axis=0)
            near = rows_of[at, :] if pooled else hint[at, :].astype(F32)
            rounded = (vec - near).astype(BF16)
            res = rounded.astype(F32)
            both[at, :] = vec.astype(BF16)
            both[low, :] = rounded
            along = jnp.sum(vec * res, axis=1, keepdims=True)
            energy = 1e-06 + jnp.sum(res * res, axis=1, keepdims=True)
            stats[0, at, :] = jnp.broadcast_to(along, (2 * MINE, LANES))
            stats[1, at, :] = jnp.broadcast_to((1.0 / 32.0) / energy, (2 * MINE, LANES))
            return carry

        lax.fori_loop(0, mine.shape[0], prepare, 0, unroll=mine.shape[0])
        first += mine.shape[0]
    stats[2] = jnp.full((rows, LANES), -jnp.inf, F32)
    stats[3] = jnp.zeros((rows, LANES), F32)
    held_b[...] = jnp.full_like(held_b, -1e30)
    held_b[rows:, :] = jnp.zeros((rows, STEP), F32)

    def product(held, t):
        part = pl.ds(pl.multiple_of(t * STEP, STEP), STEP)
        held[...] = dot_t(both[...], table[part, :])

    def settle(held, t):
        first = pl.multiple_of(t * STEP, STEP)
        for g in range(0, rows, 8):
            at, low = slice(g, g + 8), slice(rows + g, rows + g + 8)
            along, weight, peak = stats[0, at, :], stats[1, at, :], stats[2, at, :]
            parts = []
            for j in range(0, STEP, LANES):
                cols = pl.ds(first + j, LANES)
                gap = along - held[low, j : j + LANES]
                part = held[at, j : j + LANES] * (1.0 / 16.0) - norms[:, cols] - gap * gap * weight
                made[at, cols] = part
                parts.append(part)
            new = functools.reduce(jnp.maximum, parts, peak)
            sums = [jnp.exp(part - new) for part in parts]
            while len(sums) > 1:
                sums = [sums[i] + sums[i + 1] for i in range(0, len(sums), 2)]
            stats[3, at, :] = stats[3, at, :] * jnp.exp(peak - new) + sums[0]
            stats[2, at, :] = new

    def turn(i, carry):
        bring(2 * i).wait()
        bring(2 * i + 1).wait()

        @pl.when(i + 1 < n // 2)
        def _():
            bring(2 * i + 2).start()
            bring(2 * i + 3).start()

        product(held_a, 2 * i)
        settle(held_b, jnp.maximum(2 * i - 1, 0))
        product(held_b, 2 * i + 1)
        settle(held_a, 2 * i)

        @pl.when(i > 0)
        def _():
            give_all(2 * i - 1)

        give_all(2 * i)
        return carry

    lax.fori_loop(0, n // 2, turn, 0)
    settle(held_b, n - 1)
    give_all(n - 1)
    for r in range(X):
        at = slice(r * LANES, (r + 1) * LANES)
        peak = stats[2, at, :]
        top = jnp.max(peak, axis=1, keepdims=True)
        total = jnp.sum(stats[3, at, :] * jnp.exp(peak - top), axis=1, keepdims=True)
        column = jnp.broadcast_to(top + jnp.log(total), (LANES, LANES))
        lse[pl.ds((where[1] + r) & (X - 1), 1), :] = jnp.transpose(column)[:1]
    for t in range(n):
        for r in range(X):
            give(t, r).wait()


def finish_kernel(k_all, every, held, out, done, shift, sems):
    rows, k_dev = out.shape
    n = sems.shape[0]
    block = rows // n

    def give(t):
        part = pl.ds(t * block, block)
        return pltpu.make_async_copy(done.at[part, :], out.at[part, :], sems.at[t])

    for r in range(every.shape[1]):
        each = every[:, r]
        peak = jnp.max(each, axis=0, keepdims=True)
        total = jnp.sum(jnp.exp(each - peak), axis=0, keepdims=True)
        row = peak + jnp.log(total) - jnp.log(jnp.full((1, LANES), k_all, F32))
        shift[r * LANES : (r + 1) * LANES, :] = jnp.transpose(jnp.broadcast_to(row, (LANES, LANES)))
    for t in range(n):

        def group(g, carry):
            at = pl.ds(pl.multiple_of(t * block + g * 16, 16), 16)
            less = shift[at, :]
            for j in range(0, k_dev, LANES):
                done[at, j : j + LANES] = (held[at, j : j + LANES] - less).astype(BF16)
            return carry

        lax.fori_loop(0, block // 16, group, 0)
        give(t).start()
    for t in range(n):
        give(t).wait()


def collect(where, ids, cent):
    rows = ids.shape[0] * MINE
    k_dev, dim = cent.shape
    part = jax.ShapeDtypeStruct((HALF, dim), BF16)
    return pl.pallas_call(
        collect_kernel,
        out_shape=(part, part, jax.ShapeDtypeStruct((rows, LANES), I32), jax.ShapeDtypeStruct((1,), I32)),
        in_specs=[IN_SMEM, IN_VMEM, IN_PLACE],
        out_specs=(IN_VMEM, IN_VMEM, IN_VMEM, IN_SMEM),
        scratch_shapes=[
            pltpu.VMEM((SLOTS, dim), F32),
            pltpu.VMEM((SLOTS, 16, dim), BF16),
            pltpu.VMEM((8, LANES), I32),
            pltpu.SMEM((8, LANES), I32),
            pltpu.SemaphoreType.DMA((SLOTS,)),
            pltpu.SemaphoreType.DMA,
        ],
        compiler_params=PARAMS,
        name="collect",
    )(where, ids, cent)


def norms_of(cent):
    k_dev, dim = cent.shape
    return pl.pallas_call(
        norms_kernel,
        grid=(4,),
        out_shape=jax.ShapeDtypeStruct((1, k_dev), F32),
        in_specs=[pl.BlockSpec((k_dev // 4, dim), lambda i: (i, 0))],
        out_specs=pl.BlockSpec((1, k_dev // 4), lambda i: (0, i)),
        compiler_params=PARAMS,
        cost_estimate=pl.CostEstimate(flops=4 * cent.size, bytes_accessed=2 * cent.size, transcendentals=0),
        name="norms",
    )(cent)


def scores(pooled, where, blocks, hint, norms, cent):
    k_dev, dim = cent.shape
    rows = hint.shape[0]
    chips = rows // (2 * MINE)
    n = k_dev // STEP
    return pl.pallas_call(
        functools.partial(score_kernel, pooled),
        out_shape=(
            jax.ShapeDtypeStruct((rows, k_dev), F32),
            jax.ShapeDtypeStruct((X, LANES), F32),
        ),
        in_specs=[IN_SMEM] + [IN_VMEM] * (len(blocks) + 2) + [IN_PLACE],
        out_specs=(IN_PLACE, IN_VMEM),
        scratch_shapes=[
            pltpu.VMEM((2 * chips * HALF, dim), BF16),
            pltpu.VMEM((rows, dim), F32),
            pltpu.VMEM((2 * rows, dim), BF16),
            pltpu.VMEM((k_dev, dim), BF16),
            pltpu.VMEM((rows, k_dev), F32),
            pltpu.VMEM((2 * rows, STEP), F32),
            pltpu.VMEM((2 * rows, STEP), F32),
            pltpu.VMEM((4, rows, LANES), F32),
            pltpu.SemaphoreType.DMA((n,)),
            pltpu.SemaphoreType.DMA((n * X,)),
        ],
        compiler_params=PARAMS,
        name="score",
    )(where, *blocks, hint, norms, cent)


def finish(k_all, every, held):
    rows, k_dev = held.shape
    n = 8
    return pl.pallas_call(
        functools.partial(finish_kernel, k_all),
        out_shape=jax.ShapeDtypeStruct((rows, k_dev), BF16),
        in_specs=[IN_VMEM, IN_VMEM],
        out_specs=IN_PLACE,
        scratch_shapes=[
            pltpu.VMEM((rows, k_dev), BF16),
            pltpu.VMEM((rows, LANES), F32),
            pltpu.SemaphoreType.DMA((n,)),
        ],
        compiler_params=SMALL,
        name="finish",
    )(every, pltpu.with_memory_space_constraint(held, pltpu.VMEM))


def send_to_all(block, axes):
    n = lax.axis_size(axes)
    return lax.all_to_all(jnp.broadcast_to(block[None], (n,) + block.shape), axes, 0, 0, tiled=True)


def primaries(core, offset, ids, cent):
    k_dev, dim = cent.shape
    chips = lax.axis_size(CHIPS)
    local = ids[:, 0].reshape(chips, 2, MINE) - offset
    local = jnp.where(core == 0, local, local[:, ::-1])
    local = jnp.swapaxes(local, 0, 1).reshape(-1, 1)
    hot = (local == lax.broadcasted_iota(I32, (1, k_dev), 1)).astype(BF16)
    found = jnp.dot(hot, cent, preferred_element_type=F32).astype(BF16).reshape(2, chips, MINE, dim)
    for_me = found[0] + lax.ppermute(found[1], "core", SWAP)
    parts = lax.all_to_all(for_me, CHIPS, 0, 0, tiled=True)
    mine = jnp.sum(parts.astype(F32), axis=0).astype(BF16)
    own = send_to_all(mine, CHIPS)
    other = lax.ppermute(own, "core", SWAP)
    pair = jnp.stack([jnp.where(core == 0, own, other), jnp.where(core == 0, other, own)], axis=1)
    return pair.reshape(-1, dim)


def body(vectors, primary, centroids):
    k_dev, dim = centroids.shape
    owners = lax.axis_size(CENT)
    core, x = lax.axis_index("core"), lax.axis_index("x")
    offset = lax.axis_index(CENT) * k_dev
    where = jnp.stack([core, x, offset, lax.axis_index(CHIPS)]).astype(I32)

    ids = send_to_all(primary.reshape(1, MINE), CENT)
    ids, norms = lax.optimization_barrier((ids, norms_of(centroids)))

    keep, away, place, most = collect(where, ids, centroids)
    slots = keep + lax.ppermute(away, "core", SWAP)
    column = send_to_all(jnp.concatenate([slots, vectors], axis=0), "z")
    up = [(i, (i + 1) % X) for i in range(X)]
    down = [(i, (i - 1) % X) for i in range(X)]
    after, before = lax.ppermute(column, "x", down), lax.ppermute(column, "x", up)
    middle = column.shape[0] // 2
    far = lax.ppermute(before[:middle], "x", up), lax.ppermute(after[middle:], "x", down)
    own = (column, after, *far, before)
    blocks = (*own, *(lax.ppermute(block, "core", SWAP) for block in own))

    def dense():
        near = primaries(core, offset, ids, centroids).reshape(X, -1, dim)
        near = jnp.take(near, (x + jnp.arange(X)) % X, axis=0).reshape(-1, dim)
        return scores(False, where, blocks, near, norms, centroids)

    score, lse = lax.cond(
        most[0] < SLOTS, lambda: scores(True, where, blocks, place, norms, centroids), dense
    )
    every = send_to_all(lse, CENT)
    return finish(k_dev * owners, every, score)


def solution(mesh):
    fine = Mesh(mesh.devices.reshape(4, 8, 2, 4), CENT + ("slab",))
    return jax.shard_map(
        body,
        mesh=fine,
        in_specs=(P(("slab",) + CENT, None), P(("slab",) + CENT), P(CENT, None)),
        out_specs=P("slab", CENT),
        check_vma=False,
    )
```

```python
import functools

import jax
import jax.numpy as jnp
from jax import lax
from jax.experimental import pallas as pl
from jax.experimental.pallas import tpu as pltpu
from jax.sharding import Mesh, PartitionSpec as P

CENT = ("x", "z", "core")
CHIPS = ("x", "z")
SWAP = [(0, 1), (1, 0)]
F32 = jnp.float32
BF16 = jnp.bfloat16
I32 = jnp.int32
IN_VMEM = pl.BlockSpec(memory_space=pltpu.VMEM)
IN_SMEM = pl.BlockSpec(memory_space=pltpu.SMEM)
IN_PLACE = pl.BlockSpec(memory_space=pl.ANY)
PARAMS = pltpu.CompilerParams(vmem_limit_bytes=60 * 1024 * 1024)
SMALL = pltpu.CompilerParams(vmem_limit_bytes=24 * 1024 * 1024)
LANES = 128
X = 4
MINE = 8
STEP = 512
HALF = 16
SLOTS = 2 * HALF


def dot_t(a, b):
    return lax.dot_general(a, b, (((1,), (1,)), ((), ())), preferred_element_type=F32)


def collect_kernel(where, ids, cent, keep, away, place, most, found, stage, named, named_too, sems, sem):
    k_dev, dim = cent.shape
    rows = place.shape[0]
    owners = rows // MINE
    core = where[0]

    row = lax.broadcasted_iota(I32, (owners, MINE, MINE), 1)
    lane = lax.broadcasted_iota(I32, (owners, MINE, MINE), 2)
    each = jnp.broadcast_to(ids[...].astype(F32), (owners, MINE, MINE))
    column = jnp.sum(jnp.where(row == lane, each, 0.0), axis=2, keepdims=True).reshape(rows, 1)
    column = jnp.broadcast_to(column, (rows, LANES))
    chip = jnp.floor(column * (0.5 / k_dev))
    rank = jnp.zeros((rows, LANES), F32)
    before = lax.broadcasted_iota(I32, (rows, LANES), 0)
    after = lax.broadcasted_iota(I32, (rows, LANES), 1)
    for r in range(0, rows, LANES):
        across = jnp.transpose(chip[r : r + LANES])[:1]
        rank = rank + jnp.where((chip == across) & (after + r < before), 1.0, 0.0)
    rank = jnp.broadcast_to(jnp.sum(rank, axis=1, keepdims=True).astype(I32), (rows, LANES))
    here = (rank == after) & (chip.astype(I32) == where[3])
    slot = jnp.sum(jnp.where(here, column + 1.0, 0.0), axis=0, keepdims=True).astype(I32) - 1
    named[...] = jnp.broadcast_to(slot, named.shape)
    tell = pltpu.make_async_copy(named, named_too, sem)
    tell.start()

    half = lax.shift_right_logical(rank, 4) ^ core
    spot = chip.astype(I32)
    spot = ((lax.shift_right_logical(spot, 3) - where[1]) & 3) * 8 + (spot & 7)
    at = half * (rows // (2 * MINE) * HALF) + spot * HALF + (rank & (HALF - 1))
    for r in range(X):
        to = pl.multiple_of(((r - where[1]) & (X - 1)) * LANES, LANES)
        place[pl.ds(to, LANES), :] = at[r * LANES : (r + 1) * LANES]
    most[0] = jnp.max(rank)
    found[...] = jnp.zeros_like(found)
    tell.wait()

    def is_mine(s):
        local = named_too[0, s] - where[2]
        return (local >= 0) & (local < k_dev)

    def bring(s):
        group = pl.multiple_of((named_too[0, s] - where[2]) // 16 * 16, 16)
        return pltpu.make_async_copy(cent.at[pl.ds(group, 16), :], stage.at[s], sems.at[s])

    def start(s, carry):
        @pl.when(is_mine(s))
        def _():
            bring(s).start()

        return carry

    def take(s, carry):
        @pl.when(is_mine(s))
        def _():
            bring(s).wait()
            row = lax.broadcasted_iota(I32, (16, dim), 0)
            inside = lax.rem(named_too[0, s] - where[2], 16)
            picked = jnp.where(row == inside, stage[s].astype(F32), 0.0)
            found[pl.ds(s, 1), :] = jnp.sum(picked, axis=0, keepdims=True)

        return carry

    lax.fori_loop(0, SLOTS, start, 0)
    lax.fori_loop(0, SLOTS, take, 0)
    keep[...] = found[pl.ds(pl.multiple_of(core * HALF, HALF), HALF), :].astype(BF16)
    away[...] = found[pl.ds(pl.multiple_of((1 - core) * HALF, HALF), HALF), :].astype(BF16)


def norms_kernel(cent, norms):
    for r in range(0, cent.shape[0], LANES):
        wide = cent[r : r + LANES, :].astype(F32)
        column = jnp.sum(wide * wide, axis=1, keepdims=True) * (1.0 / 32.0)
        norms[:, r : r + LANES] = jnp.transpose(jnp.broadcast_to(column, (LANES, LANES)))[:1]


def score_kernel(pooled, where, *refs):
    own, other = refs[:8], refs[8:16]
    hint, norms, cent, score, lse, pool, rows_of, both, table, made, held_a, held_b, stats, in_sems, out_sems = refs[16:]
    dim = cent.shape[1]
    chips = sum(ref.shape[0] for ref in own)
    rows = 2 * chips * MINE
    k_dev = cent.shape[0]
    n = k_dev // STEP
    core = where[0]

    def bring(t):
        part = pl.ds(pl.multiple_of(t * STEP, STEP), STEP)
        return pltpu.make_async_copy(cent.at[part, :], table.at[part, :], in_sems.at[t])

    def give(t, r):
        part = pl.ds(pl.multiple_of(t * STEP, STEP), STEP)
        to = pl.ds(pl.multiple_of(((where[1] + r) & (X - 1)) * LANES, LANES), LANES)
        return pltpu.make_async_copy(
            made.at[r * LANES : (r + 1) * LANES, part], score.at[to, part], out_sems.at[t * X + r]
        )

    def give_all(t):
        for r in range(X):
            give(t, r).start()

    bring(0).start()
    bring(1).start()
    if pooled:
        spot = 0
        for ref in (*own, *other):
            for z in range(ref.shape[0]):
                pool[spot : spot + HALF, :] = ref[z, :HALF, :]
                spot += HALF
        lane = lax.broadcasted_iota(I32, (rows, LANES), 1)
        hot = [(hint[...] == lane + j).astype(F32).astype(BF16) for j in range(0, 2 * chips * HALF, LANES)]
        rows_of[...] = jnp.dot(jnp.concatenate(hot, axis=1), pool[...], preferred_element_type=F32)

    first = 0
    for mine, theirs in zip(own, other, strict=True):

        def prepare(z, carry, mine=mine, theirs=theirs, first=first):
            at = pl.ds(pl.multiple_of((first + z) * 2 * MINE, 2 * MINE), 2 * MINE)
            low = pl.ds(pl.multiple_of(rows + (first + z) * 2 * MINE, 2 * MINE), 2 * MINE)
            a = mine[z, HALF : HALF + MINE, :].astype(F32)
            b = theirs[z, HALF : HALF + MINE, :].astype(F32)
            vec = jnp.concatenate([jnp.where(core == 0, a, b), jnp.where(core == 0, b, a)], axis=0)
            near = rows_of[at, :] if pooled else hint[at, :].astype(F32)
            rounded = (vec - near).astype(BF16)
            res = rounded.astype(F32)
            both[at, :] = vec.astype(BF16)
            both[low, :] = rounded
            along = jnp.sum(vec * res, axis=1, keepdims=True)
            energy = 1e-06 + jnp.sum(res * res, axis=1, keepdims=True)
            stats[0, at, :] = jnp.broadcast_to(along, (2 * MINE, LANES))
            stats[1, at, :] = jnp.broadcast_to((1.0 / 32.0) / energy, (2 * MINE, LANES))
            return carry

        lax.fori_loop(0, mine.shape[0], prepare, 0, unroll=4)
        first += mine.shape[0]
    stats[2] = jnp.full((rows, LANES), -jnp.inf, F32)
    stats[3] = jnp.zeros((rows, LANES), F32)
    held_b[...] = jnp.full_like(held_b, -1e30)
    held_b[rows:, :] = jnp.zeros((rows, STEP), F32)

    def product(held, t):
        part = pl.ds(pl.multiple_of(t * STEP, STEP), STEP)
        held[...] = dot_t(both[...], table[part, :])

    def settle(held, t):
        first = pl.multiple_of(t * STEP, STEP)
        for g in range(0, rows, 8):
            at, low = slice(g, g + 8), slice(rows + g, rows + g + 8)
            along, weight, peak = stats[0, at, :], stats[1, at, :], stats[2, at, :]
            parts = []
            for j in range(0, STEP, LANES):
                cols = pl.ds(first + j, LANES)
                gap = along - held[low, j : j + LANES]
                part = held[at, j : j + LANES] * (1.0 / 16.0) - norms[:, cols] - gap * gap * weight
                made[at, cols] = part
                parts.append(part)
            new = functools.reduce(jnp.maximum, parts, peak)
            sums = [jnp.exp(part - new) for part in parts]
            while len(sums) > 1:
                sums = [sums[i] + sums[i + 1] for i in range(0, len(sums), 2)]
            stats[3, at, :] = stats[3, at, :] * jnp.exp(peak - new) + sums[0]
            stats[2, at, :] = new

    def turn(i, carry):
        bring(2 * i).wait()
        bring(2 * i + 1).wait()

        @pl.when(i + 1 < n // 2)
        def _():
            bring(2 * i + 2).start()
            bring(2 * i + 3).start()

        product(held_a, 2 * i)
        settle(held_b, jnp.maximum(2 * i - 1, 0))
        product(held_b, 2 * i + 1)
        settle(held_a, 2 * i)

        @pl.when(i > 0)
        def _():
            give_all(2 * i - 1)

        give_all(2 * i)
        return carry

    lax.fori_loop(0, n // 2, turn, 0)
    settle(held_b, n - 1)
    give_all(n - 1)
    for r in range(X):
        at = slice(r * LANES, (r + 1) * LANES)
        peak = stats[2, at, :]
        top = jnp.max(peak, axis=1, keepdims=True)
        total = jnp.sum(stats[3, at, :] * jnp.exp(peak - top), axis=1, keepdims=True)
        column = jnp.broadcast_to(top + jnp.log(total), (LANES, LANES))
        lse[pl.ds((where[1] + r) & (X - 1), 1), :] = jnp.transpose(column)[:1]
    for t in range(n):
        for r in range(X):
            give(t, r).wait()


def finish_kernel(k_all, every, held, out, done, shift, sems):
    rows, k_dev = out.shape
    n = sems.shape[0]
    block = rows // n

    def give(t):
        part = pl.ds(t * block, block)
        return pltpu.make_async_copy(done.at[part, :], out.at[part, :], sems.at[t])

    for r in range(every.shape[1]):
        each = every[:, r]
        peak = jnp.max(each, axis=0, keepdims=True)
        total = jnp.sum(jnp.exp(each - peak), axis=0, keepdims=True)
        row = peak + jnp.log(total) - jnp.log(jnp.full((1, LANES), k_all, F32))
        shift[r * LANES : (r + 1) * LANES, :] = jnp.transpose(jnp.broadcast_to(row, (LANES, LANES)))
    for t in range(n):

        def group(g, carry):
            at = pl.ds(pl.multiple_of(t * block + g * 16, 16), 16)
            less = shift[at, :]
            for j in range(0, k_dev, LANES):
                done[at, j : j + LANES] = (held[at, j : j + LANES] - less).astype(BF16)
            return carry

        lax.fori_loop(0, block // 16, group, 0)
        give(t).start()
    for t in range(n):
        give(t).wait()


def collect(where, ids, cent):
    rows = ids.shape[0] * MINE
    k_dev, dim = cent.shape
    part = jax.ShapeDtypeStruct((HALF, dim), BF16)
    return pl.pallas_call(
        collect_kernel,
        out_shape=(part, part, jax.ShapeDtypeStruct((rows, LANES), I32), jax.ShapeDtypeStruct((1,), I32)),
        in_specs=[IN_SMEM, IN_VMEM, IN_PLACE],
        out_specs=(IN_VMEM, IN_VMEM, IN_VMEM, IN_SMEM),
        scratch_shapes=[
            pltpu.VMEM((SLOTS, dim), F32),
            pltpu.VMEM((SLOTS, 16, dim), BF16),
            pltpu.VMEM((8, LANES), I32),
            pltpu.SMEM((8, LANES), I32),
            pltpu.SemaphoreType.DMA((SLOTS,)),
            pltpu.SemaphoreType.DMA,
        ],
        compiler_params=PARAMS,
        name="collect",
    )(where, ids, cent)


def norms_of(cent):
    k_dev, dim = cent.shape
    return pl.pallas_call(
        norms_kernel,
        grid=(4,),
        out_shape=jax.ShapeDtypeStruct((1, k_dev), F32),
        in_specs=[pl.BlockSpec((k_dev // 4, dim), lambda i: (i, 0))],
        out_specs=pl.BlockSpec((1, k_dev // 4), lambda i: (0, i)),
        compiler_params=PARAMS,
        cost_estimate=pl.CostEstimate(flops=4 * cent.size, bytes_accessed=2 * cent.size, transcendentals=0),
        name="norms",
    )(cent)


def scores(pooled, where, blocks, hint, norms, cent):
    k_dev, dim = cent.shape
    rows = hint.shape[0]
    chips = rows // (2 * MINE)
    n = k_dev // STEP
    return pl.pallas_call(
        functools.partial(score_kernel, pooled),
        out_shape=(
            jax.ShapeDtypeStruct((rows, k_dev), F32),
            jax.ShapeDtypeStruct((X, LANES), F32),
        ),
        in_specs=[IN_SMEM] + [IN_VMEM] * (len(blocks) + 2) + [IN_PLACE],
        out_specs=(IN_PLACE, IN_VMEM),
        scratch_shapes=[
            pltpu.VMEM((2 * chips * HALF, dim), BF16),
            pltpu.VMEM((rows, dim), F32),
            pltpu.VMEM((2 * rows, dim), BF16),
            pltpu.VMEM((k_dev, dim), BF16),
            pltpu.VMEM((rows, k_dev), F32),
            pltpu.VMEM((2 * rows, STEP), F32),
            pltpu.VMEM((2 * rows, STEP), F32),
            pltpu.VMEM((4, rows, LANES), F32),
            pltpu.SemaphoreType.DMA((n,)),
            pltpu.SemaphoreType.DMA((n * X,)),
        ],
        compiler_params=PARAMS,
        name="score",
    )(where, *blocks, hint, norms, cent)


def finish(k_all, every, held):
    rows, k_dev = held.shape
    n = 4
    return pl.pallas_call(
        functools.partial(finish_kernel, k_all),
        out_shape=jax.ShapeDtypeStruct((rows, k_dev), BF16),
        in_specs=[IN_VMEM, IN_VMEM],
        out_specs=IN_PLACE,
        scratch_shapes=[
            pltpu.VMEM((rows, k_dev), BF16),
            pltpu.VMEM((rows, LANES), F32),
            pltpu.SemaphoreType.DMA((n,)),
        ],
        compiler_params=SMALL,
        name="finish",
    )(every, pltpu.with_memory_space_constraint(held, pltpu.VMEM))


def send_to_all(block, axes):
    n = lax.axis_size(axes)
    return lax.all_to_all(jnp.broadcast_to(block[None], (n,) + block.shape), axes, 0, 0, tiled=True)


def primaries(core, offset, ids, cent):
    k_dev, dim = cent.shape
    chips = lax.axis_size(CHIPS)
    local = ids[:, 0].reshape(chips, 2, MINE) - offset
    local = jnp.where(core == 0, local, local[:, ::-1])
    local = jnp.swapaxes(local, 0, 1).reshape(-1, 1)
    hot = (local == lax.broadcasted_iota(I32, (1, k_dev), 1)).astype(BF16)
    found = jnp.dot(hot, cent, preferred_element_type=F32).astype(BF16).reshape(2, chips, MINE, dim)
    for_me = found[0] + lax.ppermute(found[1], "core", SWAP)
    parts = lax.all_to_all(for_me, CHIPS, 0, 0, tiled=True)
    mine = jnp.sum(parts.astype(F32), axis=0).astype(BF16)
    own = send_to_all(mine, CHIPS)
    other = lax.ppermute(own, "core", SWAP)
    pair = jnp.stack([jnp.where(core == 0, own, other), jnp.where(core == 0, other, own)], axis=1)
    return pair.reshape(-1, dim)


def body(vectors, primary, centroids):
    k_dev, dim = centroids.shape
    owners = lax.axis_size(CENT)
    core, x = lax.axis_index("core"), lax.axis_index("x")
    offset = lax.axis_index(CENT) * k_dev
    where = jnp.stack([core, x, offset, lax.axis_index(CHIPS)]).astype(I32)

    ids = send_to_all(primary.reshape(1, MINE), CENT)
    ids, norms = lax.optimization_barrier((ids, norms_of(centroids)))

    keep, away, place, most = collect(where, ids, centroids)
    slots = keep + lax.ppermute(away, "core", SWAP)
    column = send_to_all(jnp.concatenate([slots, vectors], axis=0), "z")
    up = [(i, (i + 1) % X) for i in range(X)]
    down = [(i, (i - 1) % X) for i in range(X)]
    middle = column.shape[0] // 2
    low, high = column[:middle], column[middle:]
    before_low, after_high = lax.ppermute(low, "x", up), lax.ppermute(high, "x", down)
    before_high, after_low = lax.ppermute(high, "x", up), lax.ppermute(low, "x", down)
    far_low, far_high = lax.ppermute(before_low, "x", up), lax.ppermute(after_high, "x", down)
    own = (low, high, after_low, after_high, far_low, far_high, before_low, before_high)
    blocks = (*own, *(lax.ppermute(block, "core", SWAP) for block in own))

    def dense():
        near = primaries(core, offset, ids, centroids).reshape(X, -1, dim)
        near = jnp.take(near, (x + jnp.arange(X)) % X, axis=0).reshape(-1, dim)
        return scores(False, where, blocks, near, norms, centroids)

    score, lse = lax.cond(
        most[0] < SLOTS, lambda: scores(True, where, blocks, place, norms, centroids), dense
    )
    every = send_to_all(lse, CENT)
    return finish(k_dev * owners, every, score)


def solution(mesh):
    fine = Mesh(mesh.devices.reshape(4, 8, 2, 4), CENT + ("slab",))
    return jax.shard_map(
        body,
        mesh=fine,
        in_specs=(P(("slab",) + CENT, None), P(("slab",) + CENT), P(CENT, None)),
        out_specs=P("slab", CENT),
        check_vma=False,
    )
```
